512 devices in a mesh: section: 32 (over y, x_lo, core), dp: 16 (over z, x_hi).
Axes of the slice: x: 4 (x_hi: 2, x_lo: 2; x = x_hi * 2 + x_lo), y: 8, z: 8, core: 2. Of those that a mesh axis runs over, the one named last changes fastest.
Arguments:
- queries: bfloat16 [32, 2048, 2048], P('section', 'dp'), may hold values from -200 to 200, as said below
- key_values: bfloat16 [32, 1024, 4096], P('section', 'dp'), may hold values from -8 to 8, as said below
- d_context: bfloat16 [32, 2048, 2048], P('section', 'dp'), may hold values from -6 to 6
- w_kv: bfloat16 [32, 4096, 4096], P('section', 'dp'), may hold values from -0.09375 to 0.09375
- enc_len: int32 [16], P('dp'), may hold values from 32 to 64
Outputs:
- query_grads: bfloat16 [32, 2048, 2048], P('section', 'dp')
- encoder_grad: float32 [1024, 4096], P('section', 'dp')
The draws below stay inside these ranges and needn't reach their ends.
Inputs may be any that keep to these rules, and one draw needn't show every extreme that they name: queries: entries stay within the range. `key_values`: entries stay within the range.
All inputs are finite; a program needn't handle non-finite values.
Results may differ from the reference program's by a relative error of at most 0.0074.
Values may be sent and summed in bfloat16 or wider, within the bound.
A program may use at most 64 MiB of HBM per device.

```python
import jax
import jax.numpy as jnp
from jax import lax

D = 4096
HEADS = 8
HEAD_DIM = 256
TDEC = 128
SENC = 64
SECTIONS = 32
MICRO = 16


def shared_keys(key):
    return jax.random.normal(jax.random.fold_in(key, 101), (SECTIONS, MICRO, SENC, HEADS, HEAD_DIM), jnp.float32)


def draw_queries(key, part):
    key = jax.random.fold_in(key, 1)
    base = jax.random.normal(key, (SECTIONS, MICRO, TDEC, HEADS, HEAD_DIM), jnp.float32)
    base = jnp.clip(base, -200.0, 200.0)
    return base.reshape(SECTIONS, MICRO * TDEC, HEADS * HEAD_DIM).astype(jnp.bfloat16)


def draw_key_values(key, part):
    keys_base = shared_keys(key)
    key = jax.random.fold_in(key, 3)
    values = jax.random.normal(key, (SECTIONS, MICRO, SENC, HEADS, HEAD_DIM), jnp.float32)
    keys_all = keys_base
    keys_all = jnp.clip(keys_all, -8.0, 8.0)
    values = jnp.clip(values, -8.0, 8.0)
    keys_flat = keys_all.reshape(SECTIONS, MICRO * SENC, HEADS * HEAD_DIM)
    values_flat = values.reshape(SECTIONS, MICRO * SENC, HEADS * HEAD_DIM)
    return jnp.concatenate([keys_flat, values_flat], axis=2).astype(jnp.bfloat16)


def set_ends(values, stream_key, low, largest):
    extent = values.shape
    place = [jax.random.randint(jax.random.fold_in(stream_key, axis), (), 0, extent[axis]) for axis in range(len(extent))]
    values = values.at[tuple(place)].set(low)
    longest = extent.index(max(extent))
    place[longest] = (place[longest] + 1) % extent[longest]
    return values.at[tuple(place)].set(largest)


def block_scale(rng, dims, pieces, smallest, largest):
    def one(position, parts):
        steps = jax.random.uniform(jax.random.fold_in(jax.random.fold_in(rng, 6), position), (parts,), jnp.float32, smallest / len(pieces), largest / len(pieces))
        return jnp.repeat(jnp.exp(steps), dims[position] // parts).reshape((-1,) + (1,) * (len(dims) - position - 1))

    loudness = one(*pieces[0])
    for cut in pieces[1:]:
        loudness = loudness * one(*cut)
    return loudness


def scatter_about(rng, dims, deviation, reach, cuts=(), kind=jnp.bfloat16):
    result = deviation * jax.random.normal(rng, dims, jnp.float32)
    if cuts:
        result = result * block_scale(rng, dims, cuts, -0.22, 0.18)
    return jnp.clip(result, -reach, reach).astype(kind)


def setup_inputs(seed: int = 0) -> dict:
    key_of = jax.random.split(jax.random.key(seed), 6)
    queries = draw_queries(jax.random.fold_in(key_of[5], 71), 0)
    key_values = draw_key_values(jax.random.fold_in(key_of[5], 71), 0)
    d_context = scatter_about(key_of[2], (SECTIONS, MICRO * TDEC, HEADS * HEAD_DIM), 1.0, 6.0, ((0, 32), (1, 16)))
    w_kv = scatter_about(key_of[3], (SECTIONS, D, 2 * HEADS * HEAD_DIM), (2 * HEADS * HEAD_DIM) ** -0.5, 0.09375, ((0, 32), (1, 16)))
    enc_len = set_ends(jax.random.randint(key_of[4], (MICRO,), SENC // 2, SENC + 1), jax.random.fold_in(key_of[4], 1), SENC // 2, SENC).astype(jnp.int32)
    return dict(queries=queries, key_values=key_values, d_context=d_context, w_kv=w_kv, enc_len=enc_len)


def attend_back(queries, key_values, d_context, enc_len):
    width = HEADS * HEAD_DIM
    micro = queries.shape[0] // TDEC
    scale = HEAD_DIM ** -0.5
    qfull = queries.reshape(micro, TDEC, HEADS, HEAD_DIM).astype(jnp.float32)
    kfull = key_values[:, :width].reshape(micro, SENC, HEADS, HEAD_DIM).astype(jnp.float32)
    vfull = key_values[:, width:].reshape(micro, SENC, HEADS, HEAD_DIM).astype(jnp.float32)
    dfull = d_context.reshape(micro, TDEC, HEADS, HEAD_DIM).astype(jnp.float32)
    scores = jnp.einsum("mthe,mshe->mhts", qfull, kfull) * scale
    places = jnp.arange(SENC, dtype=jnp.int32)
    live = places[None, None, None, :] < enc_len[:, None, None, None]
    scores = jnp.where(live, scores, -1e9)
    peak = jnp.max(scores, axis=-1, keepdims=True)
    expo = jnp.exp(scores - peak)
    probs = expo / jnp.sum(expo, axis=-1, keepdims=True)
    probs_low = probs.astype(jnp.bfloat16).astype(jnp.float32)
    context = jnp.einsum("mhts,mshe->mthe", probs_low, vfull)
    delta = jnp.sum(dfull * context, axis=-1)
    delta = jnp.transpose(delta, (0, 2, 1))[..., None]
    dprobs = jnp.einsum("mthe,mshe->mhts", dfull, vfull)
    dscores = (probs * (dprobs - delta)).astype(jnp.bfloat16).astype(jnp.float32)
    dquery = (jnp.einsum("mhts,mshe->mthe", dscores, kfull) * scale).astype(jnp.bfloat16)
    dkey = (jnp.einsum("mhts,mthe->mshe", dscores, qfull) * scale).astype(jnp.bfloat16)
    dvalue = jnp.einsum("mhts,mthe->mshe", probs_low, dfull).astype(jnp.bfloat16)
    dquery = dquery.reshape(micro * TDEC, width)
    dkey = dkey.reshape(micro * SENC, width)
    dvalue = dvalue.reshape(micro * SENC, width)
    return dquery, dkey, dvalue


def reference(queries, key_values, d_context, w_kv, enc_len):
    def one_layer(total, layer):
        q_layer, kv_layer, d_layer, w_layer = layer
        dquery, dkey, dvalue = attend_back(q_layer, kv_layer, d_layer, enc_len)
        kv_grads = jnp.concatenate([dkey, dvalue], axis=1)
        term = lax.dot_general(kv_grads, w_layer, (((1,), (1,)), ((), ())), preferred_element_type=jnp.float32)
        return total + term, dquery

    start = jnp.zeros((MICRO * SENC, D), jnp.float32)
    encoder_grad, query_grads = lax.scan(one_layer, start, (queries, key_values, d_context, w_kv))
    return query_grads, encoder_grad
```

```python
import functools

import jax
import jax.numpy as jnp
from jax import lax
from jax.experimental import pallas as pl
from jax.experimental.pallas import tpu as pltpu
from jax.sharding import PartitionSpec as P

MESH = pl.DeviceIdType.MESH
BF = jnp.bfloat16
F32 = jnp.float32
HEADS = 8
HALF = HEADS // 2
HD = 256
TDEC = 128
SENC = 64
WIDTH = HEADS * HD
RING = 8
SCALE = HD ** (-0.5)


def dot_nt(a, b):
    return lax.dot_general(a, b, (((1,), (1,)), ((), ())), preferred_element_type=F32)


def dot_nn(a, b):
    return lax.dot_general(a, b, (((1,), (0,)), ((), ())), preferred_element_type=F32)


def dot_tn(a, b):
    return lax.dot_general(a, b, (((0,), (0,)), ((), ())), preferred_element_type=F32)


def kernel(
    len_ref, q_ref, kv_ref, do_ref, w_ref, dq_ref, eg_ref,
    g, xs, wv, asend, abuf, bsend, bbuf,
    wl_sem, ws_sem, wr_sem, xs_sem, xr_sem, zs_sem, zr_sem, as_sem, ar_sem, bs_sem, br_sem,
):
    section, dp = lax.axis_index("section"), lax.axis_index("dp")
    y, xl, c = section // 4, (section // 2) % 2, section % 2
    z, xh = dp // 2, dp % 2

    def device(y, xl, c, z, xh):
        return (y * 4 + xl * 2 + c, z * 2 + xh)

    def around(k):
        return device(y, (xl + k // 4) % 2, (c + (k // 2) % 2) % 2, z, (xh + k % 2) % 2)

    barrier = pltpu.get_barrier_semaphore()
    for up in (1, RING - 1):
        pl.semaphore_signal(barrier, inc=1, device_id=device(y, xl, c, (z + up) % RING, xh), device_id_type=MESH)
    for k in range(1, 8):
        pl.semaphore_signal(barrier, inc=1, device_id=around(k), device_id_type=MESH)
        pl.semaphore_signal(barrier, inc=1, device_id=device((y + k) % RING, xl, c, z, xh), device_id_type=MESH)

    def w_columns(half, hh, part):
        return pl.ds(pl.multiple_of(part * WIDTH + (half * HALF + hh) * HD, HD), HD)

    def w_local(hh, part):
        return pltpu.make_async_copy(
            w_ref.at[:, w_columns(xh, hh, part)],
            wv.at[hh, pl.ds(0, HD), pl.ds(part * HD, HD)],
            wl_sem.at[hh, part],
        )

    def w_remote(hh, part):
        return pltpu.make_async_remote_copy(
            src_ref=w_ref.at[:, w_columns(1 - xh, hh, part)],
            dst_ref=wv.at[hh, pl.ds(HD, HD), pl.ds(part * HD, HD)],
            send_sem=ws_sem.at[hh, part],
            recv_sem=wr_sem.at[hh, part],
            device_id=around(1),
            device_id_type=MESH,
        )

    for hh in range(HALF):
        for part in range(2):
            w_local(hh, part).start()

    def x_copy(hh):
        return pltpu.make_async_remote_copy(
            src_ref=xs.at[hh],
            dst_ref=g.at[0, hh, pl.ds(SENC, SENC)],
            send_sem=xs_sem.at[hh],
            recv_sem=xr_sem.at[hh],
            device_id=around(1),
            device_id_type=MESH,
        )

    def z_copy(s, d, r, hh):
        source = g.at[0, hh, pl.ds(r * SENC, SENC)] if s == 1 else g.at[2 * s - 3 + r, hh, pl.ds(d * SENC, SENC)]
        place = g.at[7, hh, pl.ds(r * SENC, SENC)] if s == 4 else g.at[2 * s - 1 + r, hh, pl.ds(d * SENC, SENC)]
        return pltpu.make_async_remote_copy(
            src_ref=source,
            dst_ref=place,
            send_sem=zs_sem.at[s - 1, d, r, hh],
            recv_sem=zr_sem.at[s - 1, d, r, hh],
            device_id=device(y, xl, c, (z + (1 if d == 0 else RING - 1)) % RING, xh),
            device_id_type=MESH,
        )

    live = lax.broadcasted_iota(jnp.int32, (SENC, TDEC), 0) < len_ref[0]

    def head(index):
        cols = pl.ds(pl.multiple_of(index * HD, HD), HD)
        vcols = pl.ds(pl.multiple_of(WIDTH + index * HD, HD), HD)
        q, k, v, do = q_ref[:, cols], kv_ref[:, cols], kv_ref[:, vcols], do_ref[:, cols]
        scores = jnp.where(live, dot_nt(k, q) * SCALE, -1e9)
        expo = jnp.exp(scores - jnp.max(scores, axis=0, keepdims=True))
        probs = expo / jnp.sum(expo, axis=0, keepdims=True)
        probs_low = probs.astype(BF)
        dprobs = dot_nt(v, do)
        delta = jnp.sum(probs_low.astype(F32) * dprobs, axis=0, keepdims=True)
        dscores = (probs * (dprobs - delta)).astype(BF)
        dq_ref[:, cols] = (dot_tn(dscores, k) * SCALE).astype(BF)
        dk = (dot_nn(dscores, q) * SCALE).astype(BF)
        dv = dot_nn(probs_low, do).astype(BF)
        return dk, dv

    def pair(hh):
        dk, dv = head(xh * HALF + hh)
        g[0, hh, :SENC, :HD] = dk
        g[0, hh, :SENC, HD:] = dv
        dk, dv = head((1 - xh) * HALF + hh)
        xs[hh, :, :HD] = dk
        xs[hh, :, HD:] = dv

    def send_pair(hh):
        z_copy(1, 0, 0, hh).start()
        z_copy(1, 1, 0, hh).start()
        x_copy(hh).start()

    pair(0)
    pl.semaphore_wait(barrier, 16)
    send_pair(0)

    def more(hh, _):
        pair(hh)
        send_pair(hh)
        return 0

    lax.fori_loop(1, HALF, more, 0)

    for hh in range(HALF):
        for part in range(2):
            w_remote(hh, part).start()

    def from_partner(hh, _):
        x_copy(hh).wait_recv()
        z_copy(1, 0, 1, hh).start()
        z_copy(1, 1, 1, hh).start()
        return 0

    lax.fori_loop(0, HALF, from_partner, 0)

    def pass_on(s, r, hh):
        z_copy(s, 0, r, hh).wait_recv()
        if s < 3 or r == 0:
            z_copy(s + 1, 0, r, hh).start()
        z_copy(s, 1, r, hh).wait_recv()
        if s < 3 or r == 1:
            z_copy(s + 1, 1, r, hh).start()

    for s in (1, 2):
        for r in (0, 1):
            lax.fori_loop(0, HALF, lambda hh, _, s=s, r=r: (pass_on(s, r, hh), 0)[1], 0)

    for hh in range(HALF):
        for part in range(2):
            w_local(hh, part).wait()
            w_remote(hh, part).wait_recv()

    def product(t):
        total = dot_nt(g[t, 0], wv[0])
        for hh in range(1, HALF):
            total += dot_nt(g[t, hh], wv[hh])
        return total.astype(BF)

    def product_ring(t):
        total = product(t)
        group, r = (t + 1) // 2, (t + 1) % 2
        for d in range(2):
            for j in range(2):
                for n in range(2):
                    at = d * 64 + j * 32
                    asend[group, r * 4 + j * 2 + n, d * 32 : d * 32 + 32, :] = total[at : at + 32, n * HD : n * HD + HD]

    def product_edge(t, group):
        total = product(t)
        for r in range(2):
            for j in range(2):
                for n in range(2):
                    at = r * 64 + j * 32
                    asend[group, r * 4 + j * 2 + n, :32, :] = total[at : at + 32, n * HD : n * HD + HD]

    def a_piece(k):
        return ((xl + k // 4 + xh) % 2) * 4 + ((c + (k // 2) % 2) % 2) * 2 + k % 2

    def a_copy(group, k):
        rows = pl.ds(0, 32 if group in (0, 4) else 64)
        return pltpu.make_async_remote_copy(
            src_ref=asend.at[group, a_piece(k), rows],
            dst_ref=abuf.at[group, k, rows],
            send_sem=as_sem.at[group, k],
            recv_sem=ar_sem.at[group, k],
            device_id=around(k),
            device_id_type=MESH,
        )

    def a_start(group):
        for k in range(1, 8):
            a_copy(group, k).start()

    def b_place(group, d):
        return (z + (group if d == 1 else RING - group)) % RING

    def b_copy(group, d):
        return pltpu.make_async_remote_copy(
            src_ref=bsend.at[group, pl.ds(d * 32, 32)],
            dst_ref=bbuf.at[y],
            send_sem=bs_sem.at[group, d],
            recv_sem=br_sem.at[y],
            device_id=device(b_place(group, d), xl, c, z, xh),
            device_id_type=MESH,
        )

    def gather_sum(group):
        rows = 32 if group in (0, 4) else 64
        total = asend[group, a_piece(0), :rows, :].astype(F32)
        for k in range(1, 8):
            a_copy(group, k).wait_recv()
            total += abuf[group, k, :rows, :].astype(F32)
        bsend[group, :rows, :] = total
        for d in range(rows // 32):
            away = b_place(group, d) != y

            @pl.when(away)
            def _():
                b_copy(group, d).start()

            @pl.when(jnp.logical_not(away))
            def _():
                bbuf[y] = total[d * 32 : d * 32 + 32]

    def last_hop(r, hh):
        pass_on(3, r, hh)

    def step_a(hh, _):
        last_hop(0, hh)
        product_ring(1 + hh)
        return 0

    lax.fori_loop(0, 2, step_a, 0)
    a_start(1)
    lax.fori_loop(2, 4, step_a, 0)
    a_start(2)
    last_hop(1, 0)
    product_edge(0, 0)
    a_start(0)
    last_hop(1, 1)
    product_ring(5)
    last_hop(1, 2)
    gather_sum(1)
    last_hop(1, 3)
    product_ring(6)
    a_start(3)
    gather_sum(2)
    gather_sum(0)

    for r in range(2):
        lax.fori_loop(0, HALF, lambda hh, _, r=r: (z_copy(4, r, r, hh).wait_recv(), 0)[1], 0)
    product_edge(7, 4)
    a_start(4)
    gather_sum(3)
    gather_sum(4)

    for hh in range(HALF):
        x_copy(hh).wait_send()
        for part in range(2):
            w_remote(hh, part).wait_send()

    def sent(hh, _):
        for s in (1, 2, 3):
            for d in range(2):
                for r in range(2):
                    z_copy(s, d, r, hh).wait_send()
        for r in range(2):
            z_copy(4, r, r, hh).wait_send()
        return 0

    lax.fori_loop(0, HALF, sent, 0)
    for group in range(5):
        for k in range(1, 8):
            a_copy(group, k).wait_send()
        for d in range(1 if group in (0, 4) else 2):

            @pl.when(b_place(group, d) != y)
            def _():
                b_copy(group, d).wait_send()

    for k in range(1, RING):
        other = (y + k) % RING
        pltpu.make_async_remote_copy(
            src_ref=bsend.at[0, pl.ds(0, 32)],
            dst_ref=bbuf.at[other],
            send_sem=bs_sem.at[0, 0],
            recv_sem=br_sem.at[other],
            device_id=device(other, xl, c, z, xh),
            device_id_type=MESH,
        ).wait_recv()
    total = bbuf[0]
    for k in range(1, RING):
        total += bbuf[k]
    eg_ref[...] = total


def local(queries, key_values, d_context, w_kv, enc_len):
    vmem = pl.BlockSpec(memory_space=pltpu.VMEM)
    dma = pltpu.SemaphoreType.DMA
    dquery, encoder_grad = pl.pallas_call(
        kernel,
        out_shape=(
            jax.ShapeDtypeStruct((TDEC, WIDTH), BF),
            jax.ShapeDtypeStruct((32, HD), F32),
        ),
        in_specs=[pl.BlockSpec(memory_space=pltpu.SMEM), vmem, vmem, vmem, pl.BlockSpec(memory_space=pl.ANY)],
        out_specs=(vmem, vmem),
        scratch_shapes=[
            pltpu.VMEM((8, HALF, 2 * SENC, 2 * HD), BF),
            pltpu.VMEM((HALF, SENC, 2 * HD), BF),
            pltpu.VMEM((HALF, 2 * HD, 2 * HD), BF),
            pltpu.VMEM((5, 8, 64, HD), BF),
            pltpu.VMEM((5, 8, 64, HD), BF),
            pltpu.VMEM((5, 64, HD), F32),
            pltpu.VMEM((RING, 32, HD), F32),
            dma((HALF, 2)), dma((HALF, 2)), dma((HALF, 2)),
            dma((HALF,)), dma((HALF,)),
            dma((4, 2, 2, HALF)), dma((4, 2, 2, HALF)),
            dma((5, 8)), dma((5, 8)),
            dma((5, 2)), dma((RING,)),
        ],
        compiler_params=pltpu.CompilerParams(
            collective_id=0, has_side_effects=True, vmem_limit_bytes=40 * 1024 * 1024
        ),
    )(enc_len, queries[0], key_values[0], d_context[0], w_kv[0])
    return dquery[None], encoder_grad


def solution(mesh):
    in_specs = (
        P("section", "dp", None),
        P("section", "dp", None),
        P("section", "dp", None),
        P("section", "dp", None),
        P("dp"),
    )
    out_specs = (P("section", "dp", None), P("section", "dp"))
    return jax.shard_map(local, mesh=mesh, in_specs=in_specs, out_specs=out_specs, check_vma=False)
```

```python
import functools

import jax
import jax.numpy as jnp
from jax import lax
from jax.experimental import pallas as pl
from jax.experimental.pallas import tpu as pltpu
from jax.sharding import PartitionSpec as P

MESH = pl.DeviceIdType.MESH
BF = jnp.bfloat16
F32 = jnp.float32
HEADS = 8
HALF = HEADS // 2
HD = 256
TDEC = 128
SENC = 64
WIDTH = HEADS * HD
RING = 8
SCALE = HD ** (-0.5)


def dot_nt(a, b):
    return lax.dot_general(a, b, (((1,), (1,)), ((), ())), preferred_element_type=F32)


def dot_nn(a, b):
    return lax.dot_general(a, b, (((1,), (0,)), ((), ())), preferred_element_type=F32)


def dot_tn(a, b):
    return lax.dot_general(a, b, (((0,), (0,)), ((), ())), preferred_element_type=F32)


def kernel(
    len_in, q_in, kv_in, do_in, w_ref, dq_ref, eg_ref,
    q_ref, kv_ref, do_ref, g, xs, wv, asend, abuf, bsend, bbuf, len_ref,
    len_sem, in_sem, wl_sem, ws_sem, wr_sem, xs_sem, xr_sem, zs_sem, zr_sem, as_sem, ar_sem, bs_sem, br_sem,
):
    section, dp = lax.axis_index("section"), lax.axis_index("dp")
    y, xl, c = section // 4, (section // 2) % 2, section % 2
    z, xh = dp // 2, dp % 2

    def device(y, xl, c, z, xh):
        return (y * 4 + xl * 2 + c, z * 2 + xh)

    def around(k):
        return device(y, (xl + k // 4) % 2, (c + (k // 2) % 2) % 2, z, (xh + k % 2) % 2)

    def load(half):
        copies = []
        for which, (source, place, part) in enumerate(
            ((q_in, q_ref, 0), (kv_in, kv_ref, 0), (kv_in, kv_ref, 1), (do_in, do_ref, 0))
        ):
            cols = pl.ds(pl.multiple_of(part * WIDTH + (xh if half == 0 else 1 - xh) * (HALF * HD), HD), HALF * HD)
            copies.append(pltpu.make_async_copy(source.at[:, cols], place.at[:, cols], in_sem.at[half, which]))
        return copies

    barrier = pltpu.get_barrier_semaphore()
    for up in (1, RING - 1):
        pl.semaphore_signal(barrier, inc=1, device_id=device(y, xl, c, (z + up) % RING, xh), device_id_type=MESH)
    for k in range(1, 8):
        pl.semaphore_signal(barrier, inc=1, device_id=around(k), device_id_type=MESH)
        pl.semaphore_signal(barrier, inc=1, device_id=device((y + k) % RING, xl, c, z, xh), device_id_type=MESH)

    len_copy = pltpu.make_async_copy(len_in, len_ref, len_sem)
    len_copy.start()
    for half in range(2):
        for copy in load(half):
            copy.start()

    def w_columns(half, hh, part):
        return pl.ds(pl.multiple_of(part * WIDTH + (half * HALF + hh) * HD, HD), HD)

    def w_local(hh, part):
        return pltpu.make_async_copy(
            w_ref.at[:, w_columns(xh, hh, part)],
            wv.at[hh, pl.ds(0, HD), pl.ds(part * HD, HD)],
            wl_sem.at[hh, part],
        )

    def w_remote(hh, part):
        return pltpu.make_async_remote_copy(
            src_ref=w_ref.at[:, w_columns(1 - xh, hh, part)],
            dst_ref=wv.at[hh, pl.ds(HD, HD), pl.ds(part * HD, HD)],
            send_sem=ws_sem.at[hh, part],
            recv_sem=wr_sem.at[hh, part],
            device_id=around(1),
            device_id_type=MESH,
        )

    for hh in range(HALF):
        for part in range(2):
            w_local(hh, part).start()

    def x_copy(hh):
        return pltpu.make_async_remote_copy(
            src_ref=xs.at[hh],
            dst_ref=g.at[0, hh, pl.ds(SENC, SENC)],
            send_sem=xs_sem.at[hh],
            recv_sem=xr_sem.at[hh],
            device_id=around(1),
            device_id_type=MESH,
        )

    def z_copy(s, d, r, hh):
        source = g.at[0, hh, pl.ds(r * SENC, SENC)] if s == 1 else g.at[2 * s - 3 + r, hh, pl.ds(d * SENC, SENC)]
        place = g.at[7, hh, pl.ds(r * SENC, SENC)] if s == 4 else g.at[2 * s - 1 + r, hh, pl.ds(d * SENC, SENC)]
        return pltpu.make_async_remote_copy(
            src_ref=source,
            dst_ref=place,
            send_sem=zs_sem.at[s - 1, d, r, hh],
            recv_sem=zr_sem.at[s - 1, d, r, hh],
            device_id=device(y, xl, c, (z + (1 if d == 0 else RING - 1)) % RING, xh),
            device_id_type=MESH,
        )

    len_copy.wait()
    live = lax.broadcasted_iota(jnp.int32, (SENC, TDEC), 0) < len_ref[0]

    def head(index):
        cols = pl.ds(pl.multiple_of(index * HD, HD), HD)
        vcols = pl.ds(pl.multiple_of(WIDTH + index * HD, HD), HD)
        q, k, v, do = q_ref[:, cols], kv_ref[:, cols], kv_ref[:, vcols], do_ref[:, cols]
        scores = jnp.where(live, dot_nt(k, q) * SCALE, -1e9)
        expo = jnp.exp(scores - jnp.max(scores, axis=0, keepdims=True))
        probs = expo / jnp.sum(expo, axis=0, keepdims=True)
        probs_low = probs.astype(BF)
        dprobs = dot_nt(v, do)
        delta = jnp.sum(probs_low.astype(F32) * dprobs, axis=0, keepdims=True)
        dscores = (probs * (dprobs - delta)).astype(BF)
        dq_ref[:, cols] = (dot_tn(dscores, k) * SCALE).astype(BF)
        dk = (dot_nn(dscores, q) * SCALE).astype(BF)
        dv = dot_nn(probs_low, do).astype(BF)
        return dk, dv

    def own_head(hh):
        dk, dv = head(xh * HALF + hh)
        g[0, hh, :SENC, :HD] = dk
        g[0, hh, :SENC, HD:] = dv

    def other_head(hh):
        dk, dv = head((1 - xh) * HALF + hh)
        xs[hh, :, :HD] = dk
        xs[hh, :, HD:] = dv

    def send_own(hh):
        z_copy(1, 0, 0, hh).start()
        z_copy(1, 1, 0, hh).start()

    for copy in load(0):
        copy.wait()
    own_head(0)
    for copy in load(1):
        copy.wait()
    other_head(0)
    pl.semaphore_wait(barrier, 16)
    send_own(0)
    x_copy(0).start()

    def more(hh, _):
        own_head(hh)
        send_own(hh)
        other_head(hh)
        x_copy(hh).start()
        return 0

    lax.fori_loop(1, HALF, more, 0)

    for hh in range(HALF):
        for part in range(2):
            w_remote(hh, part).start()

    def from_partner(hh, _):
        x_copy(hh).wait_recv()
        z_copy(1, 0, 1, hh).start()
        z_copy(1, 1, 1, hh).start()
        return 0

    lax.fori_loop(0, HALF, from_partner, 0)

    def pass_on(s, r, hh):
        z_copy(s, 0, r, hh).wait_recv()
        if s < 3 or r == 0:
            z_copy(s + 1, 0, r, hh).start()
        z_copy(s, 1, r, hh).wait_recv()
        if s < 3 or r == 1:
            z_copy(s + 1, 1, r, hh).start()

    for s in (1, 2):
        for r in (0, 1):
            lax.fori_loop(0, HALF, lambda hh, _, s=s, r=r: (pass_on(s, r, hh), 0)[1], 0)

    for hh in range(HALF):
        for part in range(2):
            w_local(hh, part).wait()
            w_remote(hh, part).wait_recv()

    def product(t):
        total = dot_nt(g[t, 0], wv[0])
        for hh in range(1, HALF):
            total += dot_nt(g[t, hh], wv[hh])
        return total.astype(BF)

    def product_ring(t):
        total = product(t)
        group, r = (t + 1) // 2, (t + 1) % 2
        for d in range(2):
            for j in range(2):
                for n in range(2):
                    at = d * 64 + j * 32
                    asend[group, r * 4 + j * 2 + n, d * 32 : d * 32 + 32, :] = total[at : at + 32, n * HD : n * HD + HD]

    def place_edge(total, group):
        for r in range(2):
            for j in range(2):
                for n in range(2):
                    at = r * 64 + j * 32
                    asend[group, r * 4 + j * 2 + n, :32, :] = total[at : at + 32, n * HD : n * HD + HD]

    def a_piece(k):
        return ((xl + k // 4 + xh) % 2) * 4 + ((c + (k // 2) % 2) % 2) * 2 + k % 2

    def a_copy(group, k):
        rows = pl.ds(0, 32 if group in (0, 4) else 64)
        return pltpu.make_async_remote_copy(
            src_ref=asend.at[group, a_piece(k), rows],
            dst_ref=abuf.at[group, k, rows],
            send_sem=as_sem.at[group, k],
            recv_sem=ar_sem.at[group, k],
            device_id=around(k),
            device_id_type=MESH,
        )

    def a_start(group):
        for k in range(1, 8):
            a_copy(group, k).start()

    def b_place(group, d):
        return (z + (group if d == 1 else RING - group)) % RING

    def b_copy(group, d):
        return pltpu.make_async_remote_copy(
            src_ref=bsend.at[group, pl.ds(d * 32, 32)],
            dst_ref=bbuf.at[y],
            send_sem=bs_sem.at[group, d],
            recv_sem=br_sem.at[y],
            device_id=device(b_place(group, d), xl, c, z, xh),
            device_id_type=MESH,
        )

    def gather_sum(group):
        rows = 32 if group in (0, 4) else 64
        total = asend[group, a_piece(0), :rows, :].astype(F32)
        for k in range(1, 8):
            a_copy(group, k).wait_recv()
            total += abuf[group, k, :rows, :].astype(F32)
        total = total.astype(BF)
        bsend[group, :rows, :] = total
        for d in range(rows // 32):
            away = b_place(group, d) != y

            @pl.when(away)
            def _():
                b_copy(group, d).start()

            @pl.when(jnp.logical_not(away))
            def _():
                bbuf[y] = total[d * 32 : d * 32 + 32]

    def last_hop(r, hh):
        pass_on(3, r, hh)

    def step_a(hh, _):
        last_hop(0, hh)
        product_ring(1 + hh)
        return 0

    lax.fori_loop(0, 2, step_a, 0)
    a_start(1)
    lax.fori_loop(2, 4, step_a, 0)
    a_start(2)
    last_hop(1, 0)
    last_hop(1, 1)
    place_edge(product(0), 0)
    last_hop(1, 2)
    last_hop(1, 3)
    a_start(0)
    product_ring(5)
    product_ring(6)
    a_start(3)
    gather_sum(1)
    gather_sum(2)
    gather_sum(0)

    for hh in range(HALF):
        x_copy(hh).wait_send()
        for part in range(2):
            w_remote(hh, part).wait_send()

    def sent(hh, _):
        for s in (1, 2, 3):
            for d in range(2):
                for r in range(2):
                    z_copy(s, d, r, hh).wait_send()
        return 0

    lax.fori_loop(0, HALF, sent, 0)

    def a_sent(group):
        for k in range(1, 8):
            a_copy(group, k).wait_send()

    def b_sent(group):
        for d in range(1 if group in (0, 4) else 2):

            @pl.when(b_place(group, d) != y)
            def _():
                b_copy(group, d).wait_send()

    for group in range(3):
        a_sent(group)
        b_sent(group)

    far = None
    for hh in range(HALF):
        for r in range(2):
            z_copy(4, r, r, hh).wait_recv()
        part = dot_nt(g[7, hh], wv[hh])
        far = part if far is None else far + part
    place_edge(far.astype(BF), 4)
    a_start(4)
    gather_sum(3)
    for hh in range(HALF):
        for r in range(2):
            z_copy(4, r, r, hh).wait_send()
    gather_sum(4)
    for group in (3, 4):
        a_sent(group)
        b_sent(group)

    for k in range(1, RING):
        other = (y + k) % RING
        pltpu.make_async_remote_copy(
            src_ref=bsend.at[0, pl.ds(0, 32)],
            dst_ref=bbuf.at[other],
            send_sem=bs_sem.at[0, 0],
            recv_sem=br_sem.at[other],
            device_id=device(other, xl, c, z, xh),
            device_id_type=MESH,
        ).wait_recv()
    total = bbuf[0].astype(F32)
    for k in range(1, RING):
        total += bbuf[k].astype(F32)
    eg_ref[...] = total


def local(queries, key_values, d_context, w_kv, enc_len):
    vmem = pl.BlockSpec(memory_space=pltpu.VMEM)
    anywhere = pl.BlockSpec(memory_space=pl.ANY)
    dma = pltpu.SemaphoreType.DMA
    dquery, encoder_grad = pl.pallas_call(
        kernel,
        out_shape=(
            jax.ShapeDtypeStruct((TDEC, WIDTH), BF),
            jax.ShapeDtypeStruct((32, HD), F32),
        ),
        in_specs=[anywhere, anywhere, anywhere, anywhere, anywhere],
        out_specs=(vmem, vmem),
        scratch_shapes=[
            pltpu.VMEM((TDEC, WIDTH), BF),
            pltpu.VMEM((SENC, 2 * WIDTH), BF),
            pltpu.VMEM((TDEC, WIDTH), BF),
            pltpu.VMEM((8, HALF, 2 * SENC, 2 * HD), BF),
            pltpu.VMEM((HALF, SENC, 2 * HD), BF),
            pltpu.VMEM((HALF, 2 * HD, 2 * HD), BF),
            pltpu.VMEM((5, 8, 64, HD), BF),
            pltpu.VMEM((5, 8, 64, HD), BF),
            pltpu.VMEM((5, 64, HD), BF),
            pltpu.VMEM((RING, 32, HD), BF),
            pltpu.SMEM((1,), jnp.int32),
            dma, dma((2, 4)), dma((HALF, 2)), dma((HALF, 2)), dma((HALF, 2)),
            dma((HALF,)), dma((HALF,)),
            dma((4, 2, 2, HALF)), dma((4, 2, 2, HALF)),
            dma((5, 8)), dma((5, 8)),
            dma((5, 2)), dma((RING,)),
        ],
        compiler_params=pltpu.CompilerParams(
            collective_id=0, has_side_effects=True, vmem_limit_bytes=54400 * 1024
        ),
    )(enc_len, queries[0], key_values[0], d_context[0], w_kv[0])
    return dquery[None], encoder_grad


def solution(mesh):
    in_specs = (
        P("section", "dp", None),
        P("section", "dp", None),
        P("section", "dp", None),
        P("section", "dp", None),
        P("dp"),
    )
    out_specs = (P("section", "dp", None), P("section", "dp"))
    return jax.shard_map(local, mesh=mesh, in_specs=in_specs, out_specs=out_specs, check_vma=False)
```

```python
import functools

import jax
import jax.numpy as jnp
from jax import lax
from jax.experimental import pallas as pl
from jax.experimental.pallas import tpu as pltpu
from jax.sharding import PartitionSpec as P

MESH = pl.DeviceIdType.MESH
BF = jnp.bfloat16
F32 = jnp.float32
HEADS = 8
HALF = HEADS // 2
HD = 256
TDEC = 128
SENC = 64
WIDTH = HEADS * HD
RING = 8
SCALE = HD ** (-0.5)


def dot_nt(a, b):
    return lax.dot_general(a, b, (((1,), (1,)), ((), ())), preferred_element_type=F32)


def dot_nn(a, b):
    return lax.dot_general(a, b, (((1,), (0,)), ((), ())), preferred_element_type=F32)


def dot_tn(a, b):
    return lax.dot_general(a, b, (((0,), (0,)), ((), ())), preferred_element_type=F32)


def kernel(
    len_in, q_in, kv_in, do_in, w_ref, dq_ref, eg_ref,
    q_ref, kv_ref, do_ref, g, xs, wv, asend, abuf, bsend, bbuf, len_ref,
    len_sem, in_sem, wl_sem, ws_sem, wr_sem, xs_sem, xr_sem, zs_sem, zr_sem, as_sem, ar_sem, bs_sem, br_sem,
):
    section, dp = lax.axis_index("section"), lax.axis_index("dp")
    y, xl, c = section // 4, (section // 2) % 2, section % 2
    z, xh = dp // 2, dp % 2

    def device(y, xl, c, z, xh):
        return (y * 4 + xl * 2 + c, z * 2 + xh)

    def around(k):
        return device(y, (xl + k // 4) % 2, (c + (k // 2) % 2) % 2, z, (xh + k % 2) % 2)

    def load(half):
        copies = []
        for which, (source, place, part) in enumerate(
            ((q_in, q_ref, 0), (kv_in, kv_ref, 0), (kv_in, kv_ref, 1), (do_in, do_ref, 0))
        ):
            cols = pl.ds(pl.multiple_of(part * WIDTH + (xh if half == 0 else 1 - xh) * (HALF * HD), HD), HALF * HD)
            copies.append(pltpu.make_async_copy(source.at[:, cols], place.at[:, cols], in_sem.at[half, which]))
        return copies

    barrier = pltpu.get_barrier_semaphore()
    for up in (1, RING - 1):
        pl.semaphore_signal(barrier, inc=1, device_id=device(y, xl, c, (z + up) % RING, xh), device_id_type=MESH)
    for k in range(1, 8):
        pl.semaphore_signal(barrier, inc=1, device_id=around(k), device_id_type=MESH)
        pl.semaphore_signal(barrier, inc=1, device_id=device((y + k) % RING, xl, c, z, xh), device_id_type=MESH)

    len_copy = pltpu.make_async_copy(len_in, len_ref, len_sem)
    len_copy.start()
    for half in range(2):
        for copy in load(half):
            copy.start()

    def w_columns(half, hh, part):
        return pl.ds(pl.multiple_of(part * WIDTH + (half * HALF + hh) * HD, HD), HD)

    def w_local(hh, part):
        return pltpu.make_async_copy(
            w_ref.at[:, w_columns(xh, hh, part)],
            wv.at[hh, pl.ds(0, HD), pl.ds(part * HD, HD)],
            wl_sem.at[hh, part],
        )

    def w_remote(hh, part):
        return pltpu.make_async_remote_copy(
            src_ref=w_ref.at[:, w_columns(1 - xh, hh, part)],
            dst_ref=wv.at[hh, pl.ds(HD, HD), pl.ds(part * HD, HD)],
            send_sem=ws_sem.at[hh, part],
            recv_sem=wr_sem.at[hh, part],
            device_id=around(1),
            device_id_type=MESH,
        )

    for hh in range(HALF):
        for part in range(2):
            w_local(hh, part).start()

    def x_copy(hh):
        return pltpu.make_async_remote_copy(
            src_ref=xs.at[hh],
            dst_ref=g.at[0, hh, pl.ds(SENC, SENC)],
            send_sem=xs_sem.at[hh],
            recv_sem=xr_sem.at[hh],
            device_id=around(1),
            device_id_type=MESH,
        )

    def z_copy(s, d, r, hh):
        source = g.at[0, hh, pl.ds(r * SENC, SENC)] if s == 1 else g.at[2 * s - 3 + r, hh, pl.ds(d * SENC, SENC)]
        place = g.at[7, hh, pl.ds(r * SENC, SENC)] if s == 4 else g.at[2 * s - 1 + r, hh, pl.ds(d * SENC, SENC)]
        return pltpu.make_async_remote_copy(
            src_ref=source,
            dst_ref=place,
            send_sem=zs_sem.at[s - 1, d, r, hh],
            recv_sem=zr_sem.at[s - 1, d, r, hh],
            device_id=device(y, xl, c, (z + (1 if d == 0 else RING - 1)) % RING, xh),
            device_id_type=MESH,
        )

    len_copy.wait()
    live = lax.broadcasted_iota(jnp.int32, (SENC, TDEC), 0) < len_ref[0]

    def head(index):
        cols = pl.ds(pl.multiple_of(index * HD, HD), HD)
        vcols = pl.ds(pl.multiple_of(WIDTH + index * HD, HD), HD)
        q, k, v, do = q_ref[:, cols], kv_ref[:, cols], kv_ref[:, vcols], do_ref[:, cols]
        scores = jnp.where(live, dot_nt(k, q) * SCALE, -1e9)
        expo = jnp.exp(scores - jnp.max(scores, axis=0, keepdims=True))
        probs = expo / jnp.sum(expo, axis=0, keepdims=True)
        probs_low = probs.astype(BF)
        dprobs = dot_nt(v, do)
        delta = jnp.sum(probs_low.astype(F32) * dprobs, axis=0, keepdims=True)
        dscores = (probs * (dprobs - delta)).astype(BF)
        dq_ref[:, cols] = (dot_tn(dscores, k) * SCALE).astype(BF)
        dk = (dot_nn(dscores, q) * SCALE).astype(BF)
        dv = dot_nn(probs_low, do).astype(BF)
        return dk, dv

    def own_head(hh):
        dk, dv = head(xh * HALF + hh)
        g[0, hh, :SENC, :HD] = dk
        g[0, hh, :SENC, HD:] = dv

    def other_head(hh):
        dk, dv = head((1 - xh) * HALF + hh)
        xs[hh, :, :HD] = dk
        xs[hh, :, HD:] = dv

    def send_own(hh):
        z_copy(1, 0, 0, hh).start()
        z_copy(1, 1, 0, hh).start()

    for copy in load(0):
        copy.wait()
    own_head(0)
    for copy in load(1):
        copy.wait()
    other_head(0)
    pl.semaphore_wait(barrier, 16)
    send_own(0)
    x_copy(0).start()

    def more(hh, _):
        own_head(hh)
        send_own(hh)
        other_head(hh)
        x_copy(hh).start()
        return 0

    lax.fori_loop(1, HALF, more, 0)

    for hh in range(HALF):
        for part in range(2):
            w_remote(hh, part).start()

    def from_partner(hh, _):
        x_copy(hh).wait_recv()
        z_copy(1, 0, 1, hh).start()
        z_copy(1, 1, 1, hh).start()
        return 0

    lax.fori_loop(0, HALF, from_partner, 0)

    def pass_on(s, r, hh):
        z_copy(s, 0, r, hh).wait_recv()
        if s < 3 or r == 0:
            z_copy(s + 1, 0, r, hh).start()
        z_copy(s, 1, r, hh).wait_recv()
        if s < 3 or r == 1:
            z_copy(s + 1, 1, r, hh).start()

    for s in (1, 2):
        for r in (0, 1):
            lax.fori_loop(0, HALF, lambda hh, _, s=s, r=r: (pass_on(s, r, hh), 0)[1], 0)

    for hh in range(HALF):
        for part in range(2):
            w_local(hh, part).wait()
            w_remote(hh, part).wait_recv()

    def product(t):
        total = dot_nt(g[t, 0], wv[0])
        for hh in range(1, HALF):
            total += dot_nt(g[t, hh], wv[hh])
        return total.astype(BF)

    def product_ring(t):
        total = product(t)
        group, r = (t + 1) // 2, (t + 1) % 2
        for d in range(2):
            for j in range(2):
                for n in range(2):
                    at = d * 64 + j * 32
                    asend[group, r * 4 + j * 2 + n, d * 32 : d * 32 + 32, :] = total[at : at + 32, n * HD : n * HD + HD]

    def place_edge(total, group):
        for r in range(2):
            for j in range(2):
                for n in range(2):
                    at = r * 64 + j * 32
                    asend[group, r * 4 + j * 2 + n, :32, :] = total[at : at + 32, n * HD : n * HD + HD]

    def a_piece(k):
        return ((xl + k // 4 + xh) % 2) * 4 + ((c + (k // 2) % 2) % 2) * 2 + k % 2

    def a_copy(group, k):
        rows = pl.ds(0, 32 if group in (0, 4) else 64)
        return pltpu.make_async_remote_copy(
            src_ref=asend.at[group, a_piece(k), rows],
            dst_ref=abuf.at[group, k, rows],
            send_sem=as_sem.at[group, k],
            recv_sem=ar_sem.at[group, k],
            device_id=around(k),
            device_id_type=MESH,
        )

    def a_start(group):
        for k in (1, 5, 3, 7, 4, 6, 2):
            a_copy(group, k).start()

    def b_place(group, d):
        return (z + (group if d == 1 else RING - group)) % RING

    def b_copy(group, d):
        return pltpu.make_async_remote_copy(
            src_ref=bsend.at[group, pl.ds(d * 32, 32)],
            dst_ref=bbuf.at[y],
            send_sem=bs_sem.at[group, d],
            recv_sem=br_sem.at[y],
            device_id=device(b_place(group, d), xl, c, z, xh),
            device_id_type=MESH,
        )

    def gather_sum(group):
        rows = 32 if group in (0, 4) else 64
        total = asend[group, a_piece(0), :rows, :].astype(F32)
        for k in range(1, 8):
            a_copy(group, k).wait_recv()
            total += abuf[group, k, :rows, :].astype(F32)
        total = total.astype(BF)
        bsend[group, :rows, :] = total
        for d in range(rows // 32):
            away = b_place(group, d) != y

            @pl.when(away)
            def _():
                b_copy(group, d).start()

            @pl.when(jnp.logical_not(away))
            def _():
                bbuf[y] = total[d * 32 : d * 32 + 32]

    def last_hop(r, hh):
        pass_on(3, r, hh)

    def step_a(hh, _):
        last_hop(0, hh)
        product_ring(1 + hh)
        return 0

    lax.fori_loop(0, 2, step_a, 0)
    a_start(1)
    lax.fori_loop(2, 4, step_a, 0)
    a_start(2)
    last_hop(1, 0)
    last_hop(1, 1)
    place_edge(product(0), 0)
    last_hop(1, 2)
    last_hop(1, 3)
    a_start(0)
    product_ring(5)
    product_ring(6)
    a_start(3)
    gather_sum(1)
    gather_sum(2)
    gather_sum(0)

    for hh in range(HALF):
        x_copy(hh).wait_send()
        for part in range(2):
            w_remote(hh, part).wait_send()

    def sent(hh, _):
        for s in (1, 2, 3):
            for d in range(2):
                for r in range(2):
                    z_copy(s, d, r, hh).wait_send()
        return 0

    lax.fori_loop(0, HALF, sent, 0)

    def a_sent(group):
        for k in range(1, 8):
            a_copy(group, k).wait_send()

    def b_sent(group):
        for d in range(1 if group in (0, 4) else 2):

            @pl.when(b_place(group, d) != y)
            def _():
                b_copy(group, d).wait_send()

    for group in range(3):
        a_sent(group)
        b_sent(group)

    far = None
    for hh in range(HALF):
        for r in range(2):
            z_copy(4, r, r, hh).wait_recv()
        part = dot_nt(g[7, hh], wv[hh])
        far = part if far is None else far + part
    place_edge(far.astype(BF), 4)
    a_start(4)
    gather_sum(3)
    gather_sum(4)
    for hh in range(HALF):
        for r in range(2):
            z_copy(4, r, r, hh).wait_send()
    for group in (3, 4):
        a_sent(group)
        b_sent(group)

    for k in range(1, RING):
        other = (y + k) % RING
        pltpu.make_async_remote_copy(
            src_ref=bsend.at[0, pl.ds(0, 32)],
            dst_ref=bbuf.at[other],
            send_sem=bs_sem.at[0, 0],
            recv_sem=br_sem.at[other],
            device_id=device(other, xl, c, z, xh),
            device_id_type=MESH,
        ).wait_recv()
    total = bbuf[0].astype(F32)
    for k in range(1, RING):
        total += bbuf[k].astype(F32)
    eg_ref[...] = total


def write_out(dq_ref, eg_ref, dq_out, eg_out, dq_sem, eg_sem):
    dq_copy = pltpu.make_async_copy(dq_ref, dq_out, dq_sem)
    eg_copy = pltpu.make_async_copy(eg_ref, eg_out, eg_sem)
    dq_copy.start()
    eg_copy.start()
    dq_copy.wait()
    eg_copy.wait()


def local(queries, key_values, d_context, w_kv, enc_len):
    vmem = pl.BlockSpec(memory_space=pltpu.VMEM)
    anywhere = pl.BlockSpec(memory_space=pl.ANY)
    dma = pltpu.SemaphoreType.DMA
    dquery, encoder_grad = pl.pallas_call(
        kernel,
        out_shape=(
            jax.ShapeDtypeStruct((TDEC, WIDTH), BF),
            jax.ShapeDtypeStruct((32, HD), F32),
        ),
        in_specs=[anywhere, anywhere, anywhere, anywhere, anywhere],
        out_specs=(vmem, vmem),
        scratch_shapes=[
            pltpu.VMEM((TDEC, WIDTH), BF),
            pltpu.VMEM((SENC, 2 * WIDTH), BF),
            pltpu.VMEM((TDEC, WIDTH), BF),
            pltpu.VMEM((8, HALF, 2 * SENC, 2 * HD), BF),
            pltpu.VMEM((HALF, SENC, 2 * HD), BF),
            pltpu.VMEM((HALF, 2 * HD, 2 * HD), BF),
            pltpu.VMEM((5, 8, 64, HD), BF),
            pltpu.VMEM((5, 8, 64, HD), BF),
            pltpu.VMEM((5, 64, HD), BF),
            pltpu.VMEM((RING, 32, HD), BF),
            pltpu.SMEM((1,), jnp.int32),
            dma, dma((2, 4)), dma((HALF, 2)), dma((HALF, 2)), dma((HALF, 2)),
            dma((HALF,)), dma((HALF,)),
            dma((4, 2, 2, HALF)), dma((4, 2, 2, HALF)),
            dma((5, 8)), dma((5, 8)),
            dma((5, 2)), dma((RING,)),
        ],
        compiler_params=pltpu.CompilerParams(
            collective_id=0, has_side_effects=True, vmem_limit_bytes=54400 * 1024
        ),
    )(enc_len, queries[0], key_values[0], d_context[0], w_kv[0])
    dquery, encoder_grad = pl.pallas_call(
        write_out,
        out_shape=(
            jax.ShapeDtypeStruct((TDEC, WIDTH), BF),
            jax.ShapeDtypeStruct((32, HD), F32),
        ),
        in_specs=[vmem, vmem],
        out_specs=(anywhere, anywhere),
        scratch_shapes=[dma, dma],
        compiler_params=pltpu.CompilerParams(vmem_limit_bytes=54400 * 1024),
    )(dquery, encoder_grad)
    return dquery[None], encoder_grad


def solution(mesh):
    in_specs = (
        P("section", "dp", None),
        P("section", "dp", None),
        P("section", "dp", None),
        P("section", "dp", None),
        P("dp"),
    )
    out_specs = (P("section", "dp", None), P("section", "dp"))
    return jax.shard_map(local, mesh=mesh, in_specs=in_specs, out_specs=out_specs, check_vma=False)
```
